32 devices in a mesh: dp: 2 (over x), seq: 16 (over z, y, core).
Axes of the slice: x: 2, y: 2, z: 4, core: 2. Of those that a mesh axis runs over, the one named last changes fastest.
Arguments:
- tokens: bfloat16 [6144, 4096], P(('dp', 'seq')), parts along dimension 0, may hold values from -72 to 72
- monarch_inner_factor: bfloat16 [3, 64, 64, 64], replicated, may hold values from -0.75 to 0.75
- monarch_outer_factor: bfloat16 [3, 64, 64, 64], replicated, may hold values from -0.75 to 0.75
- adapter_down_weight: bfloat16 [3, 4096, 16], replicated, may hold values from -0.09375 to 0.09375
- adapter_up_weight: bfloat16 [3, 16, 4096], replicated, may hold values from -1.5 to 1.5
- pattern: int32 [96, 3], P('dp'), parts along dimension 0, may hold values from 2 to 47, as said below
Outputs:
- context: bfloat16 [6144, 4096], P(('dp', 'seq')), parts along dimension 0
The draws below stay inside these ranges and needn't reach their ends.
There are 2 independent parts, one for each index of `dp`. The reference program is written for one: setup_inputs(seed, part) draws one part's arguments, and reference() takes and returns one part's arrays. A program takes and returns all parts, laid end to end along the dimension named above; an argument that names none is the same for every part. Nothing has to cross between parts.
Inputs may be any that keep to these rules, and one draw needn't show every extreme that they name: `pattern`: row b names the random key blocks of query block b. The 9 entries of the rows of one index of seq name at most 1 block held by any one index of seq, and exactly 1 of some index's blocks. A block may be named more than once.
All inputs are finite; a program needn't handle non-finite values.
Results may differ from the reference program's by a relative error of at most 0.012.
The reference program's roundings to bfloat16 on the way count: a program that leaves them out, or rounds other values in their place, can miss the bound.
Values may be sent and summed in bfloat16 or wider, within the bound.
A program may use at most 192 MiB of HBM per device.

```python
import jax
import jax.numpy as jnp
from jax import lax

MODEL_WIDTH = 4096
HEADS = 32
HD = 128
MB = 64
ADAPTER_RANK = 16
BLK = 64
RAND = 3
GLOB_BLOCKS = 2
GLOBAL = 128
QB = 3
DOC = 3072
NB = 48
CAP = 1
N_SEQ = 16


def draw_tokens(key, part):
    values = jax.random.truncated_normal(key, -6.0, 6.0, (DOC, MODEL_WIDTH), jnp.float32)
    return values.astype(jnp.bfloat16)


def draw_pattern(key, part):
    request_count = QB * RAND

    def for_device(device):
        device_key = jax.random.fold_in(key, device)
        orderings = [jax.random.permutation(jax.random.fold_in(device_key, slot), N_SEQ) for slot in range(CAP)]
        sources = jnp.concatenate(orderings)[:request_count].astype(jnp.int32)
        raw_draw = jax.random.randint(jax.random.fold_in(device_key, CAP + 7), (request_count,), 0, 1048576, jnp.int32)
        lowest = jnp.where(sources == 0, GLOB_BLOCKS, 0).astype(jnp.int32)
        within = lowest + raw_draw % (QB - lowest)
        return sources * QB + within
    picked = jax.vmap(for_device)(jnp.arange(N_SEQ, dtype=jnp.int32))
    return picked.reshape(NB, RAND).astype(jnp.int32)


def bell_draw(stream_key, dims, deviation, reach, held_as=jnp.bfloat16):
    drawn = deviation * jax.random.normal(stream_key, dims, jnp.float32)
    return jnp.clip(drawn, min=-reach, max=reach).astype(held_as)


def setup_inputs(seed: int = 0, part: int = 0) -> dict:
    streams_of = jax.random.split(jax.random.key(seed), 7)
    part_splits = jax.random.split(jax.random.fold_in(streams_of[6], part), 7)
    tokens = draw_tokens(jax.random.fold_in(jax.random.fold_in(streams_of[6], part), 71), part)
    monarch_inner_factor = bell_draw(streams_of[1], (3, MB, MB, MB), MB ** -0.5, 0.75)
    monarch_outer_factor = bell_draw(streams_of[2], (3, MB, MB, MB), MB ** -0.5, 0.75)
    adapter_down_weight = bell_draw(streams_of[3], (3, MODEL_WIDTH, ADAPTER_RANK), MODEL_WIDTH ** -0.5, 0.09375)
    adapter_up_weight = bell_draw(streams_of[4], (3, ADAPTER_RANK, MODEL_WIDTH), ADAPTER_RANK ** -0.5, 1.5)
    pattern = draw_pattern(jax.random.fold_in(jax.random.fold_in(streams_of[6], part), 71), part)
    return dict(tokens=tokens, monarch_inner_factor=monarch_inner_factor, monarch_outer_factor=monarch_outer_factor, adapter_down_weight=adapter_down_weight, adapter_up_weight=adapter_up_weight, pattern=pattern)


def finalize_rows(values):
    return lax.optimization_barrier(values.astype(jnp.bfloat16)).astype(jnp.float32)


def apply_projection(tokens, monarch_inner_factor, monarch_outer_factor, adapter_down_weight, adapter_up_weight):
    row_count = tokens.shape[0]
    split_rows = tokens.reshape(row_count, MB, MB).astype(jnp.float32)
    inner_rows = jnp.einsum('tai,paij->ptaj', split_rows, monarch_inner_factor.astype(jnp.float32))
    main_part = jnp.einsum('ptaj,pjak->ptjk', finalize_rows(inner_rows), monarch_outer_factor.astype(jnp.float32))
    adapter_update = jnp.einsum('kg,vgj->vkj', tokens.astype(jnp.float32), adapter_down_weight.astype(jnp.float32))
    adapter_lifted_rows = jnp.einsum('bcj,bjf->bcf', finalize_rows(adapter_update), adapter_up_weight.astype(jnp.float32))
    return (main_part.reshape(3, row_count, MODEL_WIDTH) + adapter_lifted_rows).astype(jnp.bfloat16)


def attend(query_rows, key_rows, value_rows, key_valid):
    scores = jnp.einsum('qhe,khe->hqk', query_rows, key_rows) * (float(HD) ** -0.5)
    scores = jnp.where(key_valid[None, None, :], scores, -jnp.inf)
    row_peak = jnp.max(scores, axis=-1, keepdims=True)
    weights = jnp.exp(scores - row_peak)
    row_total = jnp.sum(weights, axis=-1)
    mixed_sum = jnp.einsum('hqk,khe->qhe', finalize_rows(weights), value_rows)
    result = mixed_sum / jnp.transpose(row_total)[:, :, None]
    return result.reshape(query_rows.shape[0], MODEL_WIDTH).astype(jnp.bfloat16)


def reference(tokens, monarch_inner_factor, monarch_outer_factor, adapter_down_weight, adapter_up_weight, pattern):
    projected_rows = apply_projection(tokens, monarch_inner_factor, monarch_outer_factor, adapter_down_weight, adapter_up_weight)
    query_heads = projected_rows[0].astype(jnp.float32).reshape(DOC, HEADS, HD)
    key_heads = projected_rows[1].astype(jnp.float32).reshape(DOC, HEADS, HD)
    value_heads = projected_rows[2].astype(jnp.float32).reshape(DOC, HEADS, HD)
    offsets = jnp.arange(BLK, dtype=jnp.int32)
    global_ids = jnp.arange(GLOBAL, dtype=jnp.int32)

    def one_block(block_pair):
        block_id = block_pair[0]
        picked = block_pair[1].astype(jnp.int32)
        window_blocks = block_id + jnp.arange(-1, 2, dtype=jnp.int32)
        window_valid = (window_blocks >= GLOB_BLOCKS) & (window_blocks < NB)
        window_ids = (jnp.clip(window_blocks, 0, NB - 1)[:, None] * BLK + offsets[None, :]).reshape(-1)
        random_ids = (picked[:, None] * BLK + offsets[None, :]).reshape(-1)
        key_ids = jnp.concatenate([global_ids, window_ids, random_ids]).astype(jnp.int32)
        key_valid = jnp.concatenate([global_ids >= 0, jnp.repeat(window_valid, BLK), random_ids >= 0])
        query_rows = lax.dynamic_slice_in_dim(query_heads, (block_id * BLK).astype(jnp.int32), BLK, 0)
        return attend(query_rows, key_heads[key_ids], value_heads[key_ids], key_valid)

    block_outs = lax.map(one_block, (jnp.arange(NB, dtype=jnp.int32), pattern))
    context = block_outs.reshape(DOC, MODEL_WIDTH)
    all_valid = jnp.arange(DOC, dtype=jnp.int32) >= 0
    head_rows = attend(query_heads[:GLOBAL], key_heads, value_heads, all_valid)
    return jnp.concatenate([head_rows, context[GLOBAL:]], axis=0)
```

```python
import functools

import jax
import jax.numpy as jnp
from jax import lax
from jax.experimental import pallas as pl
from jax.experimental.pallas import tpu as pltpu
from jax.sharding import PartitionSpec as P

HEADS = 32
HD = 128
BLK = 64
RAND = 3
GLOB_BLOCKS = 2
LOG2E = 1.4426950408889634


def project(tokens, inner_factor, outer_factor, down, up, groups):
    rows, width = tokens.shape
    count = inner_factor.shape[0]
    split = tokens.reshape(rows, count, count)
    inner = jnp.einsum(
        "tai,aij->taj", split, inner_factor, preferred_element_type=jnp.float32
    ).astype(jnp.bfloat16)
    low = jnp.dot(tokens, down, preferred_element_type=jnp.float32).astype(jnp.bfloat16)
    rank = low.shape[1]
    left = jnp.concatenate(
        [inner, jnp.broadcast_to(low[:, :, None], (rows, rank, count))], axis=1
    )
    lifted = jnp.transpose(up.reshape(rank, count, width // count), (1, 0, 2))
    right = jnp.concatenate([outer_factor, lifted], axis=1)
    out = jnp.einsum("taj,jak->jtk", left, right, preferred_element_type=jnp.float32)
    out = out.astype(jnp.bfloat16).reshape(groups, count // groups, rows, width // count)
    return jnp.transpose(out, (0, 2, 1, 3)).reshape(groups, rows, width // groups)


def attend_kernel(pattern_ref, q_ref, k_ref, v_ref, o_ref):
    rows = q_ref.shape[0]
    blocks = rows // BLK
    glob = GLOB_BLOCKS * BLK
    factor = float(HD) ** (-0.5) * LOG2E

    def softmax(query, keys, values, mask=None):
        scores = lax.dot_general(
            query, keys, (((1,), (1,)), ((), ())), preferred_element_type=jnp.float32
        )
        if mask is not None:
            scores = jnp.where(mask, -jnp.inf, scores)
        peak = jnp.max(scores, axis=-1, keepdims=True)
        weights = jnp.exp2((scores - peak) * factor)
        total = jnp.sum(weights, axis=-1, keepdims=True)
        mixed = jnp.dot(weights.astype(jnp.bfloat16), values, preferred_element_type=jnp.float32)
        return (mixed / total).astype(jnp.bfloat16)

    def rows_of(block):
        return pl.ds(pl.multiple_of(block * BLK, BLK), BLK)

    def one_block(block):
        picks = [block - 1, block, jnp.minimum(block + 1, blocks - 1)]
        picks += [pattern_ref[block * RAND + r] for r in range(RAND)]
        keys = jnp.concatenate([k_ref[:glob]] + [k_ref[rows_of(b)] for b in picks], axis=0)
        values = jnp.concatenate([v_ref[:glob]] + [v_ref[rows_of(b)] for b in picks], axis=0)
        place = lax.broadcasted_iota(jnp.int32, (1, keys.shape[0]), 1)
        before = (place >= glob) & (place < glob + BLK) & (block - 1 < GLOB_BLOCKS)
        after = (place >= glob + 2 * BLK) & (place < glob + 3 * BLK) & (block + 1 >= blocks)
        return softmax(q_ref[rows_of(block)], keys, values, before | after)

    o_ref[:glob] = softmax(q_ref[:glob], k_ref[...], v_ref[...])

    group = 2 if (blocks - GLOB_BLOCKS) % 2 == 0 else 1

    def body(step, carry):
        start = GLOB_BLOCKS + step * group
        outs = [one_block(start + i) for i in range(group)]
        for i in range(group):
            o_ref[rows_of(start + i)] = outs[i]
        return carry

    lax.fori_loop(0, (blocks - GLOB_BLOCKS) // group, body, 0)


def attend(pattern, query, keys, values):
    devs, rows, features = query.shape
    flat = [x.reshape(devs * rows, features) for x in (query, keys, values)]
    spec = pl.BlockSpec((devs * rows, HD), lambda h, _: (0, h))
    out = pl.pallas_call(
        attend_kernel,
        out_shape=jax.ShapeDtypeStruct(flat[0].shape, query.dtype),
        grid_spec=pltpu.PrefetchScalarGridSpec(
            num_scalar_prefetch=1,
            grid=(features // HD,),
            in_specs=[spec] * 3,
            out_specs=spec,
        ),
        compiler_params=pltpu.CompilerParams(vmem_limit_bytes=40 * 1024 * 1024),
    )(pattern, *flat)
    return out.reshape(query.shape)


def per_device(tokens, inner_factor, outer_factor, down, up, pattern):
    rows, width = tokens.shape
    devs = lax.axis_size("seq")
    swap = functools.partial(
        lax.all_to_all, axis_name="seq", split_axis=0, concat_axis=0, tiled=True
    )
    by_head = [
        swap(project(tokens, inner_factor[p], outer_factor[p], down[p], up[p], devs))
        for p in range(inner_factor.shape[0])
    ]
    mixed = attend(pattern.reshape(-1), *by_head)
    back = swap(mixed)
    return jnp.transpose(back, (1, 0, 2)).reshape(rows, width)


def solution(mesh):
    return jax.shard_map(
        per_device,
        mesh=mesh,
        in_specs=(P(("dp", "seq"), None), P(), P(), P(), P(), P("dp", None)),
        out_specs=P(("dp", "seq"), None),
        check_vma=False,
    )
```

```python
import functools

import jax
import jax.numpy as jnp
from jax import lax
from jax.experimental import pallas as pl
from jax.experimental.pallas import tpu as pltpu
from jax.sharding import PartitionSpec as P

HEADS = 32
HD = 128
BLK = 64
RAND = 3
GLOB_BLOCKS = 2
LOG2E = 1.4426950408889634


def project(tokens, inner_factor, outer_factor, down, up, groups):
    rows, width = tokens.shape
    count = inner_factor.shape[0]
    split = tokens.reshape(rows, count, count)
    inner = jnp.einsum(
        "tai,aij->taj", split, inner_factor, preferred_element_type=jnp.float32
    ).astype(jnp.bfloat16)
    low = jnp.dot(tokens, down, preferred_element_type=jnp.float32).astype(jnp.bfloat16)
    rank = low.shape[1]
    left = jnp.concatenate(
        [inner, jnp.broadcast_to(low[:, :, None], (rows, rank, count))], axis=1
    )
    lifted = jnp.transpose(up.reshape(rank, count, width // count), (1, 0, 2))
    right = jnp.concatenate([outer_factor, lifted], axis=1)
    out = jnp.einsum("taj,jak->jtk", left, right, preferred_element_type=jnp.float32)
    heads = HEADS // groups
    out = out.astype(jnp.bfloat16)
    out = out.reshape(groups, heads, count // HEADS, rows, width // count)
    return [
        jnp.transpose(out[:, h], (0, 2, 1, 3)).reshape(groups, rows, width // HEADS)
        for h in range(heads)
    ]


def attend_kernel(pattern_ref, q_ref, k_ref, v_ref, o_ref):
    rows = q_ref.shape[0]
    blocks = rows // BLK
    glob = GLOB_BLOCKS * BLK
    factor = float(HD) ** (-0.5) * LOG2E

    def softmax(query, keys, values, mask=None):
        scores = lax.dot_general(
            query, keys, (((1,), (1,)), ((), ())), preferred_element_type=jnp.float32
        )
        if mask is not None:
            scores = jnp.where(mask, -jnp.inf, scores)
        peak = jnp.max(scores, axis=-1, keepdims=True)
        weights = jnp.exp2((scores - peak) * factor)
        total = jnp.sum(weights, axis=-1, keepdims=True)
        mixed = jnp.dot(weights.astype(jnp.bfloat16), values, preferred_element_type=jnp.float32)
        return (mixed / total).astype(jnp.bfloat16)

    def rows_of(block):
        return pl.ds(pl.multiple_of(block * BLK, BLK), BLK)

    def one_block(block):
        picks = [block - 1, block, jnp.minimum(block + 1, blocks - 1)]
        picks += [pattern_ref[block * RAND + r] for r in range(RAND)]
        keys = jnp.concatenate([k_ref[:glob]] + [k_ref[rows_of(b)] for b in picks], axis=0)
        values = jnp.concatenate([v_ref[:glob]] + [v_ref[rows_of(b)] for b in picks], axis=0)
        place = lax.broadcasted_iota(jnp.int32, (1, keys.shape[0]), 1)
        before = (place >= glob) & (place < glob + BLK) & (block - 1 < GLOB_BLOCKS)
        after = (place >= glob + 2 * BLK) & (place < glob + 3 * BLK) & (block + 1 >= blocks)
        return softmax(q_ref[rows_of(block)], keys, values, before | after)

    o_ref[:glob] = softmax(q_ref[:glob], k_ref[...], v_ref[...])

    group = 2 if (blocks - GLOB_BLOCKS) % 2 == 0 else 1

    def body(step, carry):
        start = GLOB_BLOCKS + step * group
        outs = [one_block(start + i) for i in range(group)]
        for i in range(group):
            o_ref[rows_of(start + i)] = outs[i]
        return carry

    lax.fori_loop(0, (blocks - GLOB_BLOCKS) // group, body, 0)


def attend(pattern, head, keys, value_query):
    devs, rows, features = keys.shape
    tokens = devs * rows
    keys = keys.reshape(tokens, features)
    value_query = value_query.reshape(tokens, 2 * HD)
    glob = GLOB_BLOCKS * BLK
    pairs = tokens * (glob + (3 + RAND) * BLK) + glob * tokens

    def column(place):
        return pl.BlockSpec((tokens, HD), lambda _, __: (0, place))

    out = pl.pallas_call(
        attend_kernel,
        out_shape=jax.ShapeDtypeStruct((tokens, HD), keys.dtype),
        grid_spec=pltpu.PrefetchScalarGridSpec(
            num_scalar_prefetch=1,
            grid=(1,),
            in_specs=[column(1), column(head), column(0)],
            out_specs=column(0),
        ),
        compiler_params=pltpu.CompilerParams(vmem_limit_bytes=40 * 1024 * 1024),
        cost_estimate=pl.CostEstimate(
            flops=8 * pairs * HD, bytes_accessed=8 * tokens * HD, transcendentals=pairs
        ),
    )(pattern, value_query, keys, value_query)
    return out.reshape(devs, rows, HD)


def per_device(tokens, inner_factor, outer_factor, down, up, pattern):
    rows, width = tokens.shape
    devs = lax.axis_size("seq")
    heads = HEADS // devs
    swap = functools.partial(
        lax.all_to_all, axis_name="seq", split_axis=0, concat_axis=0, tiled=True
    )
    query, keys, values = (
        functools.partial(
            project, tokens, inner_factor[p], outer_factor[p], down[p], up[p], devs
        )
        for p in range(3)
    )
    keys = swap(jnp.concatenate(keys(), axis=2))
    pairs = [jnp.concatenate(both, axis=2) for both in zip(values(), query())]
    named = pattern.reshape(-1)
    arrived = keys
    mixed, back = None, []
    for h in range(heads):
        pair, arrived = lax.optimization_barrier((pairs[h], arrived))
        pair = swap(pair)
        if h:
            pair, mixed = lax.optimization_barrier((pair, mixed))
            back.append(swap(mixed))
        mixed = attend(named, h, keys, pair)
        if h:
            mixed, back[-1] = lax.optimization_barrier((mixed, back[-1]))
        arrived = pair
    back.append(swap(mixed))
    return jnp.transpose(jnp.stack(back), (2, 1, 0, 3)).reshape(rows, width)


def solution(mesh):
    return jax.shard_map(
        per_device,
        mesh=mesh,
        in_specs=(P(("dp", "seq"), None), P(), P(), P(), P(), P("dp", None)),
        out_specs=P(("dp", "seq"), None),
        check_vma=False,
    )
```
